256 devices in a mesh: tok: 16 (over x, y_lo, core), ch: 16 (over y_hi, z).
Axes of the slice: x: 4, y: 4 (y_hi: 2, y_lo: 2; y = y_hi * 2 + y_lo), z: 8, core: 2. Of those that a mesh axis runs over, the one named last changes fastest.
Arguments:
- activations: bfloat16 [4096, 8192], P('tok', 'ch'), may hold values from -25 to 25
- weight: bfloat16 [14336, 8192], P('tok', 'ch'), may hold values from -0.0625 to 0.0625
- basis: bfloat16 [1024, 8192], P(None, 'ch'), may hold values from -0.0625 to 0.0625
Outputs:
- left_factor: float32 [14336, 1024], P(('tok', 'ch'))
The draws below stay inside these ranges and needn't reach their ends.
All inputs are finite; a program needn't handle non-finite values.
Results may differ from the reference program's by a relative error of at most 0.0088.
Values sent between devices are 32-bit elements; how exact they have to be, the bound alone decides.
No kernel may reach another device: no remote copies, remote signals or barrier semaphores. Data moves between devices by JAX's collectives and lax.ppermute only.
A program may use at most 128 MiB of HBM per device.

```python
import jax
import jax.numpy as jnp
from jax import lax

IN_CH = 8192
OUT_ROWS = 14336
RANK = 1024
TOKENS = 4096


def draw_activations(key, part):
    key = jax.random.fold_in(key, 11)
    subkeys = jax.random.split(key, 4)
    position = jnp.arange(TOKENS, dtype=jnp.float32) / TOKENS
    row_scale = 10.0 ** jax.random.uniform(subkeys[0], (TOKENS, 1)) * jnp.sqrt((1.0 + 2.0 * position[:, None]) / 3.0)
    col_scale = 10.0 ** (jax.random.uniform(subkeys[1], (1, IN_CH)) * 0.5 - 0.25)
    entries = jax.random.truncated_normal(subkeys[3], -4.0, 4.0, (TOKENS, IN_CH))
    return (entries * row_scale * col_scale / 3.0).astype(jnp.bfloat16)


def steps_of(key, shape, cuts, low, top_value):
    level, own = 1.0, jax.random.fold_in(key, 6)
    for dim, parts in cuts:
        heights = jnp.exp(jax.random.uniform(jax.random.fold_in(own, dim), (parts,), jnp.float32, low / len(cuts), top_value / len(cuts)))
        level = level * jnp.repeat(heights, shape[dim] // parts).reshape([-1 if axis == dim else 1 for axis in range(len(shape))])
    return level


def bell_draw(key, dims, spread, bound, cuts=(), kind=jnp.bfloat16):
    drawn = jax.random.normal(key, dims, jnp.float32) * spread
    if len(cuts) > 0:
        drawn = steps_of(key, dims, cuts, -0.22, 0.18) * drawn
    return jnp.clip(drawn, min=-bound, max=bound).astype(kind)


def setup_inputs(seed: int = 0) -> dict:
    key_list = jax.random.split(jax.random.key(seed), 4)
    return {
        "activations": draw_activations(jax.random.fold_in(key_list[3], 71), 0),
        "weight": bell_draw(key_list[1], (OUT_ROWS, IN_CH), IN_CH ** -0.5, 0.0625, ((0, 16), (1, 16))),
        "basis": bell_draw(key_list[2], (RANK, IN_CH), IN_CH ** -0.5, 0.0625, ((1, 16),)),
    }


damping = 0.1

def reference(activations, weight, basis):
    codes = lax.dot_general(activations.astype(jnp.float32), basis.astype(jnp.float32), (((1,), (1,)), ((), ())), preferred_element_type=jnp.float32)
    gram = lax.dot_general(codes.astype(jnp.float32), codes.astype(jnp.float32), (((0,), (0,)), ((), ())), precision=lax.Precision.HIGHEST, preferred_element_type=jnp.float32)
    codes_low = codes.astype(jnp.bfloat16)
    moments = lax.dot_general(activations.astype(jnp.float32), codes_low.astype(jnp.float32), (((0,), (0,)), ((), ())), preferred_element_type=jnp.float32)
    cross = jnp.dot(weight.astype(jnp.float32), moments.astype(jnp.float32), precision=lax.Precision.HIGHEST, preferred_element_type=jnp.float32)
    ridge = damping * jnp.trace(gram) / RANK
    damped = gram + ridge * jnp.eye(RANK, dtype=jnp.float32)
    lower = jnp.linalg.cholesky(damped)
    middle = jax.scipy.linalg.solve_triangular(lower, cross.T, lower=True)
    solved = jax.scipy.linalg.solve_triangular(lower, middle, trans=1, lower=True)
    return solved.T
```

```python
import jax
import jax.numpy as jnp
from jax import lax
from jax.experimental import pallas as pl
from jax.experimental.pallas import tpu as pltpu
from jax.sharding import Mesh
from jax.sharding import PartitionSpec as P

damping = 0.1

SUB, LANE = 8, 128
AXES = (("x", 4), ("y_lo", 2), ("core", 2), ("y_hi", 2), ("z", 8))
TOK = ("x", "y_lo", "core")
PLANE = ("x", "y_lo")
CH = ("y_hi", "z")


def tree_sum(terms):
    while len(terms) > 1:
        paired = [a + b for a, b in zip(terms[::2], terms[1::2])]
        terms = paired + ([terms[-1]] if len(terms) % 2 else [])
    return terms[0]


def spread(value):
    return jnp.broadcast_to(value, (SUB, LANE))


def invert_small(entry):
    for k in range(SUB):
        inverse = 1.0 / entry[k, k]
        row = [entry[min(k, j), max(k, j)] for j in range(SUB)]
        scaled = [value * inverse for value in row]
        for i in range(SUB):
            for j in range(i, SUB):
                if i != k and j != k:
                    entry[i, j] = entry[i, j] - scaled[i] * row[j]
        for j in range(SUB):
            if j != k:
                entry[min(k, j), max(k, j)] = scaled[j]
        entry[k, k] = -inverse
    return {place: -value for place, value in entry.items()}


def invert_block(block, between=None):
    sub = lax.broadcasted_iota(jnp.int32, (SUB, LANE), 0)
    lane = lax.broadcasted_iota(jnp.int32, (SUB, LANE), 1)
    panels = LANE // SUB
    rows = [block[r * SUB : (r + 1) * SUB, :] for r in range(panels)]
    for p in range(panels):
        base = p * SUB
        panel = rows[p]
        inside = (lane >= base) & (lane < base + SUB)
        columns = [spread(panel[:, base + j : base + j + 1]) for j in range(SUB)]
        small = invert_small(
            {(i, j): spread(columns[j][i : i + 1, :]) for j in range(SUB) for i in range(j + 1)}
        )
        small_columns = []
        for j in range(SUB):
            column = small[0, j]
            for i in range(1, SUB):
                column = jnp.where(sub == i, small[min(i, j), max(i, j)], column)
            small_columns.append(column)
        wide = jnp.where(inside, jnp.where(lane - base == sub, 1.0, 0.0), panel)
        pivot = tree_sum([small_columns[j] * spread(wide[j : j + 1, :]) for j in range(SUB)])
        pivot_rows = [spread(pivot[j : j + 1, :]) for j in range(SUB)]
        for r in list(range(p + 1, panels)) + list(range(p)):
            change = tree_sum(
                [spread(rows[r][:, base + j : base + j + 1]) * pivot_rows[j] for j in range(SUB)]
            )
            rows[r] = jnp.where(inside, 0.0, rows[r]) - change
        rows[p] = pivot
        if between is not None:
            between(p)
    return rows


def split(value):
    high = value.astype(jnp.bfloat16)
    rest = value - high.astype(jnp.float32)
    middle = rest.astype(jnp.bfloat16)
    low = (rest - middle.astype(jnp.float32)).astype(jnp.bfloat16)
    return high, middle, low


def left_parts(value):
    high, middle, low = split(value)
    return jnp.concatenate([high, middle, high, middle, high, low], 1)


def right_parts(value):
    high, middle, low = split(value)
    return jnp.concatenate([high, high, middle, middle, low, high], 0)


def product(left, right):
    return jnp.dot(left, right, preferred_element_type=jnp.float32)


def inverse_kernel(gram_ref, out_ref, left_ref, right_ref, block_ref):
    size = gram_ref.shape[0]
    blocks = size // LANE
    tile = 256
    row = lax.broadcasted_iota(jnp.int32, (LANE, LANE), 0)
    column = lax.broadcasted_iota(jnp.int32, (LANE, LANE), 1)
    diagonal = row == column
    total = jnp.zeros((LANE, LANE), jnp.float32)
    for b in range(blocks):
        own = slice(b * LANE, (b + 1) * LANE)
        total = total + jnp.where(diagonal, gram_ref[own, own], 0.0)
    ridge = damping * jnp.sum(total) / size
    out_ref[...] = gram_ref[...]
    for b in range(blocks):
        own = slice(b * LANE, (b + 1) * LANE)
        out_ref[own, own] = gram_ref[own, own] + jnp.where(diagonal, ridge, 0.0)

    def keep(rows):
        for r in range(LANE // SUB):
            block_ref[r * SUB : (r + 1) * SUB, :] = rows[r]

    keep(invert_block(out_ref[0:LANE, 0:LANE]))

    def step(k, carry):
        here = pl.ds(pl.multiple_of(k * LANE, LANE), LANE)
        after = pl.ds(pl.multiple_of(lax.rem(k + 1, blocks) * LANE, LANE), LANE)
        inverse = block_ref[...]
        inverse_parts = left_parts(inverse)
        ahead = product(inverse_parts, right_parts(out_ref[here, after]))
        following = out_ref[after, after] - product(
            left_parts(out_ref[after, here]), right_parts(ahead)
        )
        for m in range(blocks):
            rows = slice(m * LANE, (m + 1) * LANE)
            left_ref[rows, :] = left_parts(out_ref[rows, here])
        left_ref[here, :] = jnp.zeros((LANE, 6 * LANE), jnp.bfloat16)
        for m in range(size // tile):
            columns = slice(m * tile, (m + 1) * tile)
            scaled = product(inverse_parts, right_parts(out_ref[here, columns]))
            right_ref[:, columns] = right_parts(scaled)
            out_ref[here, columns] = scaled
        out_ref[:, here] = jnp.zeros((size, LANE), jnp.float32)
        out_ref[here, here] = inverse
        right_ref[:, here] = right_parts(inverse)

        def update(p):
            n, m = divmod(p, size // tile)
            columns = slice(n * tile, (n + 1) * tile)
            rows = slice(m * tile, (m + 1) * tile)
            out_ref[rows, columns] = out_ref[rows, columns] - product(
                left_ref[rows, :], right_ref[:, columns]
            )

        keep(invert_block(following, update))
        return carry

    lax.fori_loop(0, blocks, step, 0)


def damped_inverse(gram):
    size = gram.shape[0]
    return pl.pallas_call(
        inverse_kernel,
        out_shape=jax.ShapeDtypeStruct((size, size), jnp.float32),
        scratch_shapes=[
            pltpu.VMEM((size, 6 * LANE), jnp.bfloat16),
            pltpu.VMEM((6 * LANE, size), jnp.bfloat16),
            pltpu.VMEM((LANE, LANE), jnp.float32),
        ],
        compiler_params=pltpu.CompilerParams(vmem_limit_bytes=40 * 2**20),
        cost_estimate=pl.CostEstimate(
            flops=12 * size**3, bytes_accessed=8 * size**2, transcendentals=0
        ),
    )(gram)


def exchange_sum(value, axes, count):
    received = lax.all_to_all(value, axes, 0, 0, tiled=True)
    return received.reshape(count, -1, value.shape[1]).sum(0)


def exchange_gather(value, axes, count):
    copies = jnp.broadcast_to(value[None], (count,) + value.shape)
    return lax.all_to_all(copies.reshape(-1, value.shape[1]), axes, 0, 0, tiled=True)


def swap(value, axis):
    return lax.ppermute(value, axis, [(0, 1), (1, 0)])


def halves(value, index):
    half = value.shape[0] // 2
    own = lax.dynamic_slice_in_dim(value, index * half, half, 0)
    return own, lax.dynamic_slice_in_dim(value, (1 - index) * half, half, 0)


def in_order(own, other, index, dim):
    return jnp.where(
        index == 0,
        jnp.concatenate([own, other], dim),
        jnp.concatenate([other, own], dim),
    )


def shards(activations, weight, basis):
    core, y_hi, z = (lax.axis_index(name) for name in ("core", "y_hi", "z"))
    partial_value = lax.dot_general(
        activations, basis, (((1,), (1,)), ((), ())), preferred_element_type=jnp.float32
    )
    rank_width = basis.shape[0]
    codes = exchange_gather(exchange_sum(partial_value, CH, 16), CH, 16)

    strip = rank_width // 8
    own_columns = lax.dynamic_slice_in_dim(codes, z * strip, strip, 1)
    other_columns = lax.dynamic_slice_in_dim(codes, y_hi * (rank_width // 2), rank_width // 2, 1)
    gram_part = lax.dot_general(
        own_columns,
        other_columns,
        (((0,), (0,)), ((), ())),
        precision=lax.Precision.HIGHEST,
        preferred_element_type=jnp.float32,
    )
    gram_part = exchange_gather(exchange_sum(gram_part, TOK, 16), TOK, 16)
    gram_rows = in_order(gram_part, swap(gram_part, "y_hi"), y_hi, 1)
    gram = lax.all_gather(gram_rows, "z", axis=0, tiled=True)

    codes_low = codes.astype(jnp.bfloat16)
    local_moments = lax.dot_general(
        activations, codes_low, (((0,), (0,)), ((), ())), preferred_element_type=jnp.float32
    )
    own, other = halves(local_moments, core)
    own = own + swap(other, "core")
    own = exchange_gather(exchange_sum(own, PLANE, 8), PLANE, 8)
    moments = in_order(own, swap(own, "core"), core, 0)

    channels = weight.shape[1]
    rows = weight.shape[0] // 16
    by_z = weight.reshape(2, 8, rows, channels).swapaxes(0, 1).reshape(-1, channels)
    rounded = lax.reduce_precision(moments, 8, 7)
    rest = moments - rounded
    rest_rounded = lax.reduce_precision(rest, 8, 7)
    parts = [rounded, rest_rounded, rest - rest_rounded]
    cross = sum(product(by_z, part.astype(jnp.bfloat16)) for part in parts)
    cross = lax.psum_scatter(cross, "z", scatter_dimension=0, tiled=True)
    own, other = halves(cross, y_hi)
    cross = own + swap(other, "y_hi")

    inverse = damped_inverse(gram)
    return jnp.dot(
        cross, inverse, precision=lax.Precision.HIGHEST, preferred_element_type=jnp.float32
    )


def solution(mesh):
    names = tuple(name for name, _ in AXES)
    fine = Mesh(mesh.devices.reshape([size for _, size in AXES]), names)
    in_specs = (P(TOK, CH), P(TOK, CH), P(None, CH))
    out_specs = P(TOK + CH, None)
    return jax.shard_map(shards, mesh=fine, in_specs=in_specs, out_specs=out_specs, check_vma=False)
```

```python
import jax
import jax.numpy as jnp
from jax import lax
from jax.experimental import pallas as pl
from jax.experimental.pallas import tpu as pltpu
from jax.sharding import Mesh
from jax.sharding import PartitionSpec as P

damping = 0.1

SUB, LANE = 8, 128
STRIP = 5
AXES = (("x", 4), ("y_lo", 2), ("core", 2), ("y_hi", 2), ("z", 8))
TOK = ("x", "y_lo", "core")
PLANE = ("x", "y_lo")
CH = ("y_hi", "z")


def tree_sum(terms):
    while len(terms) > 1:
        paired = [a + b for a, b in zip(terms[::2], terms[1::2])]
        terms = paired + ([terms[-1]] if len(terms) % 2 else [])
    return terms[0]


def spread(value):
    return jnp.broadcast_to(value, (SUB, LANE))


def invert_small(entry):
    for k in range(SUB):
        inverse = 1.0 / entry[k, k]
        row = [entry[min(k, j), max(k, j)] for j in range(SUB)]
        scaled = [value * inverse for value in row]
        for i in range(SUB):
            for j in range(i, SUB):
                if i != k and j != k:
                    entry[i, j] = entry[i, j] - scaled[i] * row[j]
        for j in range(SUB):
            if j != k:
                entry[min(k, j), max(k, j)] = scaled[j]
        entry[k, k] = -inverse
    return {place: -value for place, value in entry.items()}


def invert_block(block, between=None):
    sub = lax.broadcasted_iota(jnp.int32, (SUB, LANE), 0)
    lane = lax.broadcasted_iota(jnp.int32, (SUB, LANE), 1)
    panels = LANE // SUB
    rows = [block[r * SUB : (r + 1) * SUB, :] for r in range(panels)]
    for p in range(panels):
        base = p * SUB
        panel = rows[p]
        inside = (lane >= base) & (lane < base + SUB)
        columns = [spread(panel[:, base + j : base + j + 1]) for j in range(SUB)]
        small = invert_small(
            {(i, j): spread(columns[j][i : i + 1, :]) for j in range(SUB) for i in range(j + 1)}
        )
        small_columns = []
        for j in range(SUB):
            column = small[0, j]
            for i in range(1, SUB):
                column = jnp.where(sub == i, small[min(i, j), max(i, j)], column)
            small_columns.append(column)
        wide = jnp.where(inside, jnp.where(lane - base == sub, 1.0, 0.0), panel)
        pivot = tree_sum([small_columns[j] * spread(wide[j : j + 1, :]) for j in range(SUB)])
        pivot_rows = [spread(pivot[j : j + 1, :]) for j in range(SUB)]
        for r in list(range(p + 1, panels)) + list(range(p)):
            change = tree_sum(
                [spread(rows[r][:, base + j : base + j + 1]) * pivot_rows[j] for j in range(SUB)]
            )
            rows[r] = jnp.where(inside, 0.0, rows[r]) - change
        rows[p] = pivot
        if between is not None:
            between(p)
    return rows


def split(value):
    high = value.astype(jnp.bfloat16)
    rest = value - high.astype(jnp.float32)
    middle = rest.astype(jnp.bfloat16)
    low = (rest - middle.astype(jnp.float32)).astype(jnp.bfloat16)
    return high, middle, low


def left_parts(value):
    high, middle, low = split(value)
    return jnp.concatenate([high, middle, high, middle, high, low], 1)


def right_parts(value):
    high, middle, low = split(value)
    return jnp.concatenate([high, high, middle, middle, low, high], 0)


def product(left, right):
    return jnp.dot(left, right, preferred_element_type=jnp.float32)


def inverse_kernel(gram_ref, out_ref, left_ref, right_ref, block_ref):
    size = out_ref.shape[0]
    blocks = size // LANE
    tile = 256
    row = lax.broadcasted_iota(jnp.int32, (LANE, LANE), 0)
    column = lax.broadcasted_iota(jnp.int32, (LANE, LANE), 1)
    diagonal = row == column
    total = jnp.zeros((LANE, LANE), jnp.float32)
    for b in range(blocks):
        total = total + jnp.where(diagonal, gram_ref[b * LANE : (b + 1) * LANE, 0:LANE], 0.0)
    ridge = damping * jnp.sum(total) / size
    for a in range(blocks):
        for d in range(STRIP):
            b = (a + d) % blocks
            ours, theirs = slice(a * LANE, (a + 1) * LANE), slice(b * LANE, (b + 1) * LANE)
            block = gram_ref[ours, d * LANE : (d + 1) * LANE]
            if d == 0:
                block = block + jnp.where(diagonal, ridge, 0.0)
            out_ref[ours, theirs] = block
            if 0 < d < blocks // 2:
                out_ref[theirs, ours] = block.T

    def keep(rows):
        for r in range(LANE // SUB):
            block_ref[r * SUB : (r + 1) * SUB, :] = rows[r]

    keep(invert_block(out_ref[0:LANE, 0:LANE]))

    def step(k, carry):
        here = pl.ds(pl.multiple_of(k * LANE, LANE), LANE)
        after = pl.ds(pl.multiple_of(lax.rem(k + 1, blocks) * LANE, LANE), LANE)
        inverse = block_ref[...]
        inverse_parts = left_parts(inverse)
        ahead = product(inverse_parts, right_parts(out_ref[here, after]))
        following = out_ref[after, after] - product(
            left_parts(out_ref[after, here]), right_parts(ahead)
        )
        for m in range(blocks):
            rows = slice(m * LANE, (m + 1) * LANE)
            left_ref[rows, :] = left_parts(out_ref[rows, here])
        left_ref[here, :] = jnp.zeros((LANE, 6 * LANE), jnp.bfloat16)
        for m in range(size // tile):
            columns = slice(m * tile, (m + 1) * tile)
            scaled = product(inverse_parts, right_parts(out_ref[here, columns]))
            right_ref[:, columns] = right_parts(scaled)
            out_ref[here, columns] = scaled
        out_ref[:, here] = jnp.zeros((size, LANE), jnp.float32)
        out_ref[here, here] = inverse
        right_ref[:, here] = right_parts(inverse)

        def update(p):
            n, m = divmod(p, size // tile)
            columns = slice(n * tile, (n + 1) * tile)
            rows = slice(m * tile, (m + 1) * tile)
            out_ref[rows, columns] = out_ref[rows, columns] - product(
                left_ref[rows, :], right_ref[:, columns]
            )

        keep(invert_block(following, update))
        return carry

    lax.fori_loop(0, blocks, step, 0)


def damped_inverse(gram):
    size = gram.shape[0]
    return pl.pallas_call(
        inverse_kernel,
        out_shape=jax.ShapeDtypeStruct((size, size), jnp.float32),
        scratch_shapes=[
            pltpu.VMEM((size, 6 * LANE), jnp.bfloat16),
            pltpu.VMEM((6 * LANE, size), jnp.bfloat16),
            pltpu.VMEM((LANE, LANE), jnp.float32),
        ],
        compiler_params=pltpu.CompilerParams(vmem_limit_bytes=40 * 2**20),
        cost_estimate=pl.CostEstimate(
            flops=12 * size**3, bytes_accessed=8 * size**2, transcendentals=0
        ),
    )(gram)


def cross_kernel(core_ref, weight_ref, own_ref, other_ref, out_ref):
    width = own_ref.shape[0]
    rows = weight_ref.shape[0] // 16
    tile = 256
    core = core_ref[0]
    left = [
        weight_ref[:, pl.ds(pl.multiple_of(start * width, width), width)]
        for start in (core, 1 - core)
    ]
    left = jnp.concatenate(left, 1)
    for n in range(out_ref.shape[1] // tile):
        columns = slice(n * tile, (n + 1) * tile)
        parts = zip(split(own_ref[:, columns]), split(other_ref[:, columns]))
        result = tree_sum([product(left, jnp.concatenate(pair, 0)) for pair in parts])
        for y in range(2):
            for z in range(8):
                source, target = (y * 8 + z) * rows, (z * 2 + y) * rows
                out_ref[target : target + rows, columns] = result[source : source + rows, :]


def cross_terms(core, weight, own, other):
    whole = pl.BlockSpec(memory_space=pltpu.VMEM)
    return pl.pallas_call(
        cross_kernel,
        out_shape=jax.ShapeDtypeStruct((weight.shape[0], own.shape[1]), jnp.float32),
        in_specs=[pl.BlockSpec(memory_space=pltpu.SMEM), whole, whole, whole],
        out_specs=whole,
        compiler_params=pltpu.CompilerParams(vmem_limit_bytes=40 * 2**20),
        cost_estimate=pl.CostEstimate(
            flops=6 * weight.size * own.shape[1], bytes_accessed=8 * 2**20, transcendentals=0
        ),
    )(core.astype(jnp.int32)[None], weight, own, other)


def exchange_sum(value, axes, count):
    received = lax.all_to_all(value, axes, 0, 0, tiled=True)
    return received.reshape(count, -1, value.shape[1]).sum(0)


def exchange_gather(value, axes, count):
    copies = jnp.broadcast_to(value[None], (count,) + value.shape)
    return lax.all_to_all(copies.reshape(-1, value.shape[1]), axes, 0, 0, tiled=True)


def swap(value, axis):
    return lax.ppermute(value, axis, [(0, 1), (1, 0)])


def halves(value, index):
    half = value.shape[0] // 2
    own = lax.dynamic_slice_in_dim(value, index * half, half, 0)
    return own, lax.dynamic_slice_in_dim(value, (1 - index) * half, half, 0)


def shards(activations, weight, basis):
    core, y_hi, z = (lax.axis_index(name) for name in ("core", "y_hi", "z"))
    partial_value = lax.dot_general(
        activations, basis, (((1,), (1,)), ((), ())), preferred_element_type=jnp.float32
    )
    rank_width = basis.shape[0]
    codes = exchange_gather(exchange_sum(partial_value, CH, 16), CH, 16)

    wide = jnp.concatenate([codes, codes[:, : (STRIP - 1) * LANE]], 1)
    own_columns = lax.dynamic_slice_in_dim(wide, z * LANE, STRIP * LANE, 1)
    gram_part = lax.dot_general(
        own_columns[:, :LANE],
        own_columns,
        (((0,), (0,)), ((), ())),
        precision=lax.Precision.HIGHEST,
        preferred_element_type=jnp.float32,
    )
    gram_sum = exchange_sum(gram_part, TOK, 16)

    codes_low = codes.astype(jnp.bfloat16)
    local_moments = lax.dot_general(
        activations, codes_low, (((0,), (0,)), ((), ())), preferred_element_type=jnp.float32
    )
    own, other = halves(local_moments, core)
    own = own + swap(other, "core")
    gram_rows = exchange_gather(gram_sum, TOK, 16)
    own, gram_rows = lax.optimization_barrier((own, gram_rows))
    gram = lax.all_gather(gram_rows, "z", axis=0, tiled=True)
    own = exchange_gather(exchange_sum(own, PLANE, 8), PLANE, 8)
    cross = cross_terms(core, weight, own, swap(own, "core"))
    cross, gram = lax.optimization_barrier((cross, gram))
    cross = lax.psum_scatter(cross, "z", scatter_dimension=0, tiled=True)
    inverse = damped_inverse(gram)
    cross, inverse = lax.optimization_barrier((cross, inverse))
    own, other = halves(cross, y_hi)
    cross = own + swap(other, "y_hi")
    return jnp.dot(
        cross, inverse, precision=lax.Precision.HIGHEST, preferred_element_type=jnp.float32
    )


def solution(mesh):
    names = tuple(name for name, _ in AXES)
    fine = Mesh(mesh.devices.reshape([size for _, size in AXES]), names)
    in_specs = (P(TOK, CH), P(TOK, CH), P(None, CH))
    out_specs = P(TOK + CH, None)
    return jax.shard_map(shards, mesh=fine, in_specs=in_specs, out_specs=out_specs, check_vma=False)
```

```python
import functools

import jax
import jax.numpy as jnp
from jax import lax
from jax.experimental import pallas as pl
from jax.experimental.pallas import tpu as pltpu
from jax.sharding import Mesh
from jax.sharding import PartitionSpec as P

damping = 0.1

SUB, LANE = 8, 128
NEAR = 1
STRIP = 5
AXES = (("x", 4), ("y_lo", 2), ("core", 2), ("y_hi", 2), ("z", 8))
TOK = ("x", "y_lo", "core")
PLANE = ("x", "y_lo")
CH = ("y_hi", "z")


def tree_sum(terms):
    while len(terms) > 1:
        paired = [a + b for a, b in zip(terms[::2], terms[1::2])]
        terms = paired + ([terms[-1]] if len(terms) % 2 else [])
    return terms[0]


def spread(value):
    return jnp.broadcast_to(value, (SUB, LANE))


def invert_small(entry):
    for k in range(SUB):
        inverse = 1.0 / entry[k, k]
        row = [entry[min(k, j), max(k, j)] for j in range(SUB)]
        scaled = [value * inverse for value in row]
        for i in range(SUB):
            for j in range(i, SUB):
                if i != k and j != k:
                    entry[i, j] = entry[i, j] - scaled[i] * row[j]
        for j in range(SUB):
            if j != k:
                entry[min(k, j), max(k, j)] = scaled[j]
        entry[k, k] = -inverse
    return {place: -value for place, value in entry.items()}


def eliminate(near, pivot):
    return tree_sum([near[j] * spread(pivot[j : j + 1, :]) for j in range(SUB)])


def invert_block(block, between=None):
    sub = lax.broadcasted_iota(jnp.int32, (SUB, LANE), 0)
    lane = lax.broadcasted_iota(jnp.int32, (SUB, LANE), 1)
    panels = LANE // SUB
    rows = [block[r * SUB : (r + 1) * SUB, :] for r in range(panels)]
    for p in range(panels):
        base = p * SUB
        panel = rows[p]
        inside = (lane >= base) & (lane < base + SUB)

        def columns_of(r):
            return [spread(rows[r][:, base + j : base + j + 1]) for j in range(SUB)]

        columns = columns_of(p)
        near = {r: columns_of(r) for r in range(p + 1, min(p + 1 + NEAR, panels))}
        small = invert_small(
            {(i, j): spread(columns[j][i : i + 1, :]) for j in range(SUB) for i in range(j + 1)}
        )
        small_columns = []
        for j in range(SUB):
            column = small[0, j]
            for i in range(1, SUB):
                column = jnp.where(sub == i, small[min(i, j), max(i, j)], column)
            small_columns.append(column)
        wide = jnp.where(inside, jnp.where(lane - base == sub, 1.0, 0.0), panel)
        pivot = eliminate(small_columns, wide)
        left = jnp.concatenate(left_list(jnp.where(lane < base, -panel, panel)), 0)
        right = jnp.concatenate(right_list(pivot), 0)
        change = lax.dot_general(
            left.astype(jnp.bfloat16),
            right.astype(jnp.bfloat16),
            (((0,), (0,)), ((), ())),
            preferred_element_type=jnp.float32,
        )
        for r in range(panels):
            if r in near:
                rows[r] = jnp.where(inside, 0.0, rows[r]) - eliminate(near[r], pivot)
            elif r != p:
                rows[r] = jnp.where(inside, 0.0, rows[r]) - change[r * SUB : (r + 1) * SUB, :]
        rows[p] = pivot
        if between is not None:
            between(p)
    return rows


def split(value):
    high = value.astype(jnp.bfloat16).astype(jnp.float32)
    rest = value - high
    middle = rest.astype(jnp.bfloat16).astype(jnp.float32)
    return high, middle, rest - middle


def left_list(value):
    high, middle, low = split(value)
    return [high, middle, high, middle, high, low]


def right_list(value):
    high, middle, low = split(value)
    return [high, high, middle, middle, low, high]


def left_parts(value):
    return jnp.concatenate([part.astype(jnp.bfloat16) for part in left_list(value)], 1)


def right_parts(value):
    return jnp.concatenate([part.astype(jnp.bfloat16) for part in right_list(value)], 0)


def product(left, right):
    return jnp.dot(left, right, preferred_element_type=jnp.float32)


def inverse_kernel(
    core_ref, own_ref, other_ref, result_ref, out_ref, left_ref, right_ref, block_ref, done
):
    size = out_ref.shape[0]
    blocks = size // LANE
    tile = 256
    half = LANE // 2
    core = core_ref[0]
    row = lax.broadcasted_iota(jnp.int32, (LANE, LANE), 0)
    column = lax.broadcasted_iota(jnp.int32, (LANE, LANE), 1)
    diagonal = row == column
    for a in range(blocks):
        for d in range(STRIP):
            b = (a + d) % blocks
            place, source = slice(b * LANE, (b + 1) * LANE), slice(d * LANE, (d + 1) * LANE)
            for part_ref, index in ((own_ref, core), (other_ref, 1 - core)):
                rows = pl.ds(pl.multiple_of(a * LANE + index * half, half), half)
                out_ref[rows, place] = part_ref[a * half : (a + 1) * half, source]
    total = jnp.zeros((LANE, LANE), jnp.float32)
    for a in range(blocks):
        ours = slice(a * LANE, (a + 1) * LANE)
        total = total + jnp.where(diagonal, out_ref[ours, ours], 0.0)
        for d in range(1, blocks // 2):
            b = (a + d) % blocks
            theirs = slice(b * LANE, (b + 1) * LANE)
            out_ref[theirs, ours] = out_ref[ours, theirs].T
    ridge = damping * jnp.sum(total) / size
    for a in range(blocks):
        ours = slice(a * LANE, (a + 1) * LANE)
        out_ref[ours, ours] = out_ref[ours, ours] + jnp.where(diagonal, ridge, 0.0)

    def keep(rows):
        for r in range(LANE // SUB):
            block_ref[r * SUB : (r + 1) * SUB, :] = rows[r]

    keep(invert_block(out_ref[0:LANE, 0:LANE]))

    def pivot_rows(here, inverse):
        inverse_parts = left_parts(inverse)
        for m in range(size // tile):
            columns = slice(m * tile, (m + 1) * tile)
            scaled = product(inverse_parts, right_parts(out_ref[here, columns]))
            right_ref[:, columns] = right_parts(scaled)
            out_ref[here, columns] = scaled

    def step(k, carry):
        here = pl.ds(pl.multiple_of(k * LANE, LANE), LANE)
        after = pl.ds(pl.multiple_of((k + 1) * LANE, LANE), LANE)
        inverse = block_ref[...]
        ahead = product(left_parts(inverse), right_parts(out_ref[here, after]))
        following = out_ref[after, after] - product(
            left_parts(out_ref[after, here]), right_parts(ahead)
        )
        for m in range(blocks):
            rows = slice(m * LANE, (m + 1) * LANE)
            left_ref[rows, :] = left_parts(out_ref[rows, here])
        left_ref[here, :] = jnp.zeros((LANE, 6 * LANE), jnp.bfloat16)
        pivot_rows(here, inverse)
        out_ref[:, here] = jnp.zeros((size, LANE), jnp.float32)
        out_ref[here, here] = inverse
        right_ref[:, here] = right_parts(inverse)

        def update(p):
            m, n = divmod(p, size // tile)
            columns = slice(n * tile, (n + 1) * tile)
            rows = slice(m * tile, (m + 1) * tile)
            out_ref[rows, columns] = out_ref[rows, columns] - product(
                left_ref[rows, :], right_ref[:, columns]
            )

        keep(invert_block(following, update))
        return carry

    lax.fori_loop(0, blocks - 1, step, 0)
    end = size - LANE
    upper = pltpu.make_async_copy(out_ref.at[:end], result_ref.at[:end], done.at[0])
    upper.start()
    inverse = block_ref[...]
    pivot_rows(slice(end, size), inverse)
    out_ref[end:, end:] = inverse
    lower = pltpu.make_async_copy(out_ref.at[end:], result_ref.at[end:], done.at[1])
    lower.start()
    upper.wait()
    lower.wait()


WHOLE = pl.BlockSpec(memory_space=pltpu.VMEM)
OUTSIDE = pl.BlockSpec(memory_space=pltpu.HBM)
SCALARS = pl.BlockSpec(memory_space=pltpu.SMEM)
ROOM = pltpu.CompilerParams(vmem_limit_bytes=40 * 2**20)
MOST = pltpu.CompilerParams(vmem_limit_bytes=60 * 2**20)


def swept(core, own, other):
    size = 2 * own.shape[0]
    return pl.pallas_call(
        inverse_kernel,
        out_shape=jax.ShapeDtypeStruct((size, size), jnp.float32),
        in_specs=[SCALARS, WHOLE, WHOLE],
        out_specs=OUTSIDE,
        scratch_shapes=[
            pltpu.VMEM((size, size), jnp.float32),
            pltpu.VMEM((size, 6 * LANE), jnp.bfloat16),
            pltpu.VMEM((6 * LANE, size), jnp.bfloat16),
            pltpu.VMEM((LANE, LANE), jnp.float32),
            pltpu.SemaphoreType.DMA((2,)),
        ],
        compiler_params=MOST,
        cost_estimate=pl.CostEstimate(
            flops=12 * size**3, bytes_accessed=8 * size**2, transcendentals=0
        ),
    )(core, own, other)


def split_kernel(value_ref, high_ref, middle_ref, low_ref):
    for part_ref, part in zip((high_ref, middle_ref, low_ref), split(value_ref[...])):
        part_ref[...] = part.astype(jnp.bfloat16)


def split_rows(value):
    rows, width = value.shape
    tile = 128
    spec = pl.BlockSpec((tile, width), lambda n: (n, 0))
    part = jax.ShapeDtypeStruct(value.shape, jnp.bfloat16)
    return pl.pallas_call(
        split_kernel,
        grid=(rows // tile,),
        out_shape=(part,) * 3,
        in_specs=[spec],
        out_specs=(spec,) * 3,
        compiler_params=ROOM,
        cost_estimate=pl.CostEstimate(
            flops=8 * value.size, bytes_accessed=10 * value.size, transcendentals=0
        ),
    )(value)


def solve_kernel(own_ref, other_ref, high_ref, middle_ref, low_ref, out_ref):
    rows, width = out_ref.shape
    end = width - LANE

    def times(value, span, columns):
        left = [part.astype(jnp.bfloat16) for part in split(value)]
        by_high = product(jnp.concatenate(left, 0), high_ref[span, columns])
        by_middle = product(jnp.concatenate(left[:2], 0), middle_ref[span, columns])
        small = by_middle[rows:] + by_high[2 * rows :] + product(left[0], low_ref[span, columns])
        return by_high[:rows] + (by_high[rows : 2 * rows] + by_middle[:rows] + small)

    cross = own_ref[...] + other_ref[...]
    rest = cross[:, end:] - times(cross[:, :end], slice(0, end), slice(end, width))
    out_ref[:, end:] = times(rest, slice(end, width), slice(end, width))
    for start in range(0, end, LANE):
        columns = slice(start, start + LANE)
        out_ref[:, columns] = times(cross[:, :end], slice(0, end), columns) + times(
            rest, slice(end, width), columns
        )


def solve(own, other, parts):
    return pl.pallas_call(
        solve_kernel,
        out_shape=jax.ShapeDtypeStruct(own.shape, jnp.float32),
        in_specs=[WHOLE] * 5,
        out_specs=WHOLE,
        compiler_params=ROOM,
        cost_estimate=pl.CostEstimate(
            flops=12 * own.size * own.shape[1], bytes_accessed=7 * 2**20, transcendentals=0
        ),
    )(own, other, *parts)


def partial_kernel(place_ref, codes_ref, activations_ref, own_ref, other_ref, gram_ref, gram_other_ref, strip_ref):
    core, z = place_ref[0], place_ref[1]
    width = own_ref.shape[0]
    blocks = codes_ref.shape[1] // LANE
    half = LANE // 2
    low = codes_ref[...].astype(jnp.bfloat16)
    for part_ref, index in ((other_ref, 1 - core), (own_ref, core)):
        channels = activations_ref[:, pl.ds(pl.multiple_of(index * width, width), width)]
        part_ref[...] = contract(channels, low)

    def strip(d):
        start = pl.multiple_of(lax.rem(z + d, blocks) * LANE, LANE)
        return [part.astype(jnp.bfloat16) for part in split(codes_ref[:, pl.ds(start, LANE)])]

    ours = strip(0)
    for d in range(STRIP):
        theirs = ours if d == 0 else strip(d)
        terms = [contract(ours[i], theirs[j]) for i, j in ((2, 0), (0, 2), (1, 1), (1, 0), (0, 1), (0, 0))]
        strip_ref[:, d * LANE : (d + 1) * LANE] = functools.reduce(jnp.add, terms)
    gram_ref[...] = strip_ref[pl.ds(pl.multiple_of(core * half, half), half), :]
    gram_other_ref[...] = strip_ref[pl.ds(pl.multiple_of((1 - core) * half, half), half), :]


def contract(left, right):
    return lax.dot_general(left, right, (((0,), (0,)), ((), ())), preferred_element_type=jnp.float32)


def partial_terms(place, codes, activations):
    width = activations.shape[1] // 2
    moments = jax.ShapeDtypeStruct((width, codes.shape[1]), jnp.float32)
    gram = jax.ShapeDtypeStruct((LANE // 2, STRIP * LANE), jnp.float32)
    return pl.pallas_call(
        partial_kernel,
        out_shape=(moments, moments, gram, gram),
        in_specs=[SCALARS, WHOLE, WHOLE],
        out_specs=(WHOLE,) * 4,
        scratch_shapes=[pltpu.VMEM((LANE, STRIP * LANE), jnp.float32)],
        compiler_params=ROOM,
        cost_estimate=pl.CostEstimate(
            flops=5 * 10**8, bytes_accessed=4 * 2**20, transcendentals=0
        ),
    )(place, codes, activations)


def cross_kernel(core_ref, weight_ref, own_ref, other_ref, out_ref):
    width = own_ref.shape[0]
    rows = weight_ref.shape[0] // 16
    tile = 256
    core = core_ref[0]
    left = [
        weight_ref[:, pl.ds(pl.multiple_of(start * width, width), width)]
        for start in (core, 1 - core)
    ]
    left = jnp.concatenate(left, 1)
    for n in range(out_ref.shape[1] // tile):
        columns = slice(n * tile, (n + 1) * tile)
        parts = zip(split(own_ref[:, columns]), split(other_ref[:, columns]))
        result = tree_sum(
            [product(left, jnp.concatenate(pair, 0).astype(jnp.bfloat16)) for pair in parts]
        )
        for y in range(2):
            for z in range(8):
                source, target = (y * 8 + z) * rows, (z * 2 + y) * rows
                out_ref[target : target + rows, columns] = result[source : source + rows, :]


def cross_terms(core, weight, own, other):
    return pl.pallas_call(
        cross_kernel,
        out_shape=jax.ShapeDtypeStruct((weight.shape[0], own.shape[1]), jnp.float32),
        in_specs=[SCALARS, WHOLE, WHOLE, WHOLE],
        out_specs=WHOLE,
        compiler_params=ROOM,
        cost_estimate=pl.CostEstimate(
            flops=6 * weight.size * own.shape[1], bytes_accessed=8 * 2**20, transcendentals=0
        ),
    )(core, weight, own, other)


def exchange_sum(value, axes, count):
    received = lax.all_to_all(value, axes, 0, 0, tiled=True)
    return received.reshape(count, -1, value.shape[1]).sum(0)


def exchange_gather(value, axes, count):
    copies = jnp.broadcast_to(value[None], (count,) + value.shape)
    return lax.all_to_all(copies.reshape(-1, value.shape[1]), axes, 0, 0, tiled=True)


def swap(value, axis):
    return lax.ppermute(value, axis, [(0, 1), (1, 0)])


def halves(value, index):
    half = value.shape[0] // 2
    own = lax.dynamic_slice_in_dim(value, index * half, half, 0)
    return own, lax.dynamic_slice_in_dim(value, (1 - index) * half, half, 0)


def shards(activations, weight, basis):
    core, y_hi, z = (lax.axis_index(name) for name in ("core", "y_hi", "z"))
    partial_value = lax.dot_general(
        activations, basis, (((1,), (1,)), ((), ())), preferred_element_type=jnp.float32
    )
    codes = exchange_gather(exchange_sum(partial_value, CH, 16), CH, 16)

    here = core.astype(jnp.int32)[None]
    place = jnp.stack([core, z]).astype(jnp.int32)
    own, other, gram, gram_other = partial_terms(place, codes, activations)
    gram = gram + swap(gram_other, "core")
    own = own + swap(other, "core")
    gram = exchange_gather(exchange_sum(gram, PLANE, 8), PLANE, 8)
    own, gram = lax.optimization_barrier((own, gram))
    gram = lax.all_gather(gram, "z", axis=0, tiled=True)
    own = exchange_gather(exchange_sum(own, PLANE, 8), PLANE, 8)
    cross = cross_terms(here, weight, own, swap(own, "core"))
    cross, gram = lax.optimization_barrier((cross, gram))
    cross = lax.psum_scatter(cross, "z", scatter_dimension=0, tiled=True)
    inverse = swept(here, gram, swap(gram, "core"))
    cross, inverse = lax.optimization_barrier((cross, inverse))
    own, other = halves(cross, y_hi)
    return solve(own, swap(other, "y_hi"), split_rows(inverse))


def solution(mesh):
    names = tuple(name for name, _ in AXES)
    fine = Mesh(mesh.devices.reshape([size for _, size in AXES]), names)
    in_specs = (P(TOK, CH), P(TOK, CH), P(None, CH))
    out_specs = P(TOK + CH, None)
    return jax.shard_map(shards, mesh=fine, in_specs=in_specs, out_specs=out_specs, check_vma=False)
```

```python
import functools

import jax
import jax.numpy as jnp
from jax import lax
from jax.experimental import pallas as pl
from jax.experimental.pallas import tpu as pltpu
from jax.sharding import Mesh
from jax.sharding import PartitionSpec as P

damping = 0.1

SUB, LANE = 8, 128
STRIP = 5
AXES = (("x", 4), ("y_lo", 2), ("core", 2), ("y_hi", 2), ("z", 8))
TOK = ("x", "y_lo", "core")
PLANE = ("x", "y_lo")
CH = ("y_hi", "z")


def tree_sum(terms):
    while len(terms) > 1:
        paired = [a + b for a, b in zip(terms[::2], terms[1::2])]
        terms = paired + ([terms[-1]] if len(terms) % 2 else [])
    return terms[0]


def spread(value):
    return jnp.broadcast_to(value, (SUB, LANE))


def invert_small(entry):
    for k in range(SUB):
        inverse = 1.0 / entry[k, k]
        row = [entry[min(k, j), max(k, j)] for j in range(SUB)]
        scaled = [value * inverse for value in row]
        for i in range(SUB):
            for j in range(i, SUB):
                if i != k and j != k:
                    entry[i, j] = entry[i, j] - scaled[i] * row[j]
        for j in range(SUB):
            if j != k:
                entry[min(k, j), max(k, j)] = scaled[j]
        entry[k, k] = -inverse
    return {place: -value for place, value in entry.items()}


def combine(columns, rows):
    return tree_sum([column * row for column, row in zip(columns, rows)])


def pick(sub, values):
    pairs = [jnp.where(sub == i, values[i], values[i + 1]) for i in range(0, SUB, 2)]
    low, high = jnp.where(sub < 2, *pairs[:2]), jnp.where(sub < 6, *pairs[2:])
    return jnp.where(sub < 4, low, high)


def invert_block(block, buffer, between=None):
    sub = lax.broadcasted_iota(jnp.int32, (SUB, LANE), 0)
    lane = lax.broadcasted_iota(jnp.int32, (SUB, LANE), 1)
    panels = LANE // SUB
    rows = [block[r * SUB : (r + 1) * SUB, :] for r in range(panels)]
    for p in range(panels):
        base = p * SUB
        panel = rows[p]
        inside = (lane >= base) & (lane < base + SUB)
        offset = (p % 2) * (SUB + 2) * SUB

        def rows_of(slot, value):
            start = offset + slot * SUB
            buffer[start : start + SUB, :] = value
            return [spread(buffer[start + i : start + i + 1, :]) for i in range(SUB)]

        def columns_of(value):
            return [spread(value[:, base + j : base + j + 1]) for j in range(SUB)]

        entries = [rows_of(j, column) for j, column in enumerate(columns_of(panel))]
        small = invert_small({(i, j): entries[j][i] for j in range(SUB) for i in range(j + 1)})
        small_columns = [
            pick(sub, [small[min(i, j), max(i, j)] for i in range(SUB)]) for j in range(SUB)
        ]
        wide = jnp.where(inside, jnp.where(lane - base == sub, 1.0, 0.0), panel)
        pivot = combine(small_columns, rows_of(SUB, wide))
        left = jnp.concatenate(left_list(jnp.where(lane < base, -panel, panel)), 0)
        right = jnp.concatenate(right_list(pivot), 0)
        change = lax.dot_general(
            left.astype(jnp.bfloat16),
            right.astype(jnp.bfloat16),
            (((0,), (0,)), ((), ())),
            preferred_element_type=jnp.float32,
        )
        for r in range(panels):
            if r == p + 1:
                amount = combine(columns_of(rows[r]), rows_of(SUB + 1, pivot))
            else:
                amount = change[r * SUB : (r + 1) * SUB, :]
            if r != p:
                rows[r] = jnp.where(inside, 0.0, rows[r]) - amount
        rows[p] = pivot
        if between is not None:
            between(p)
    return rows


def split(value):
    high = value.astype(jnp.bfloat16).astype(jnp.float32)
    rest = value - high
    middle = rest.astype(jnp.bfloat16).astype(jnp.float32)
    return high, middle, rest - middle


def left_list(value):
    high, middle, low = split(value)
    return [high, middle, high, middle, high, low]


def right_list(value):
    high, middle, low = split(value)
    return [high, high, middle, middle, low, high]


def left_parts(value):
    return jnp.concatenate([part.astype(jnp.bfloat16) for part in left_list(value)], 1)


def right_parts(value):
    return jnp.concatenate([part.astype(jnp.bfloat16) for part in right_list(value)], 0)


def product(left, right):
    return jnp.dot(left, right, preferred_element_type=jnp.float32)


def inverse_kernel(
    core_ref, own_ref, other_ref, result_ref, out_ref, left_ref, right_ref, block_ref, buffer, done
):
    size = out_ref.shape[0]
    blocks = size // LANE
    tile = 256
    half = LANE // 2
    core = core_ref[0]
    row = lax.broadcasted_iota(jnp.int32, (LANE, LANE), 0)
    column = lax.broadcasted_iota(jnp.int32, (LANE, LANE), 1)
    diagonal = row == column
    for a in range(blocks):
        for d in range(STRIP):
            b = (a + d) % blocks
            place, source = slice(b * LANE, (b + 1) * LANE), slice(d * LANE, (d + 1) * LANE)
            for part_ref, index in ((own_ref, core), (other_ref, 1 - core)):
                rows = pl.ds(pl.multiple_of(a * LANE + index * half, half), half)
                out_ref[rows, place] = part_ref[a * half : (a + 1) * half, source]
    total = jnp.zeros((LANE, LANE), jnp.float32)
    for a in range(blocks):
        ours = slice(a * LANE, (a + 1) * LANE)
        total = total + jnp.where(diagonal, out_ref[ours, ours], 0.0)
        for d in range(1, blocks // 2):
            b = (a + d) % blocks
            theirs = slice(b * LANE, (b + 1) * LANE)
            out_ref[theirs, ours] = out_ref[ours, theirs].T
    ridge = damping * jnp.sum(total) / size
    for a in range(blocks):
        ours = slice(a * LANE, (a + 1) * LANE)
        out_ref[ours, ours] = out_ref[ours, ours] + jnp.where(diagonal, ridge, 0.0)

    def keep(rows):
        for r in range(LANE // SUB):
            block_ref[r * SUB : (r + 1) * SUB, :] = rows[r]

    keep(invert_block(out_ref[0:LANE, 0:LANE], buffer))

    def pivot_rows(here, inverse):
        inverse_parts = left_parts(inverse)
        for m in range(size // tile):
            columns = slice(m * tile, (m + 1) * tile)
            scaled = product(inverse_parts, right_parts(out_ref[here, columns]))
            right_ref[:, columns] = right_parts(scaled)
            out_ref[here, columns] = scaled

    def step(k, carry):
        here = pl.ds(pl.multiple_of(k * LANE, LANE), LANE)
        after = pl.ds(pl.multiple_of((k + 1) * LANE, LANE), LANE)
        inverse = block_ref[...]
        ahead = product(left_parts(inverse), right_parts(out_ref[here, after]))
        following = out_ref[after, after] - product(
            left_parts(out_ref[after, here]), right_parts(ahead)
        )
        for m in range(blocks):
            rows = slice(m * LANE, (m + 1) * LANE)
            left_ref[rows, :] = left_parts(out_ref[rows, here])
        left_ref[here, :] = jnp.zeros((LANE, 6 * LANE), jnp.bfloat16)
        pivot_rows(here, inverse)
        out_ref[:, here] = jnp.zeros((size, LANE), jnp.float32)
        out_ref[here, here] = inverse
        right_ref[:, here] = right_parts(inverse)

        def update(p):
            m, n = divmod(p, size // tile)
            columns = slice(n * tile, (n + 1) * tile)
            rows = slice(m * tile, (m + 1) * tile)
            out_ref[rows, columns] = out_ref[rows, columns] - product(
                left_ref[rows, :], right_ref[:, columns]
            )

        keep(invert_block(following, buffer, update))
        return carry

    lax.fori_loop(0, blocks - 1, step, 0)
    end = size - LANE
    upper = pltpu.make_async_copy(out_ref.at[:end], result_ref.at[:end], done.at[0])
    upper.start()
    inverse = block_ref[...]
    pivot_rows(slice(end, size), inverse)
    out_ref[end:, end:] = inverse
    lower = pltpu.make_async_copy(out_ref.at[end:], result_ref.at[end:], done.at[1])
    lower.start()
    upper.wait()
    lower.wait()


WHOLE = pl.BlockSpec(memory_space=pltpu.VMEM)
OUTSIDE = pl.BlockSpec(memory_space=pltpu.HBM)
SCALARS = pl.BlockSpec(memory_space=pltpu.SMEM)
ROOM = pltpu.CompilerParams(vmem_limit_bytes=40 * 2**20)
MOST = pltpu.CompilerParams(vmem_limit_bytes=60 * 2**20)


def swept(core, own, other):
    size = 2 * own.shape[0]
    return pl.pallas_call(
        inverse_kernel,
        out_shape=jax.ShapeDtypeStruct((size, size), jnp.float32),
        in_specs=[SCALARS, WHOLE, WHOLE],
        out_specs=OUTSIDE,
        scratch_shapes=[
            pltpu.VMEM((size, size), jnp.float32),
            pltpu.VMEM((size, 6 * LANE), jnp.bfloat16),
            pltpu.VMEM((6 * LANE, size), jnp.bfloat16),
            pltpu.VMEM((LANE, LANE), jnp.float32),
            pltpu.VMEM((2 * (SUB + 2) * SUB, LANE), jnp.float32),
            pltpu.SemaphoreType.DMA((2,)),
        ],
        compiler_params=MOST,
        cost_estimate=pl.CostEstimate(
            flops=12 * size**3, bytes_accessed=8 * size**2, transcendentals=0
        ),
    )(core, own, other)


def split_kernel(value_ref, high_ref, middle_ref, low_ref):
    for part_ref, part in zip((high_ref, middle_ref, low_ref), split(value_ref[...])):
        part_ref[...] = part.astype(jnp.bfloat16)


def split_rows(value):
    rows, width = value.shape
    tile = 128
    spec = pl.BlockSpec((tile, width), lambda n: (n, 0))
    part = jax.ShapeDtypeStruct(value.shape, jnp.bfloat16)
    return pl.pallas_call(
        split_kernel,
        grid=(rows // tile,),
        out_shape=(part,) * 3,
        in_specs=[spec],
        out_specs=(spec,) * 3,
        compiler_params=ROOM,
        cost_estimate=pl.CostEstimate(
            flops=8 * value.size, bytes_accessed=10 * value.size, transcendentals=0
        ),
    )(value)


def solve_kernel(own_ref, other_ref, high_ref, middle_ref, low_ref, out_ref):
    rows, width = out_ref.shape
    end = width - LANE

    def times(value, span, columns):
        left = [part.astype(jnp.bfloat16) for part in split(value)]
        by_high = product(jnp.concatenate(left, 0), high_ref[span, columns])
        by_middle = product(jnp.concatenate(left[:2], 0), middle_ref[span, columns])
        small = by_middle[rows:] + by_high[2 * rows :] + product(left[0], low_ref[span, columns])
        return by_high[:rows] + (by_high[rows : 2 * rows] + by_middle[:rows] + small)

    cross = own_ref[...] + other_ref[...]
    tile = 2 * LANE
    upper, lower = slice(0, end), slice(end, width)
    final = slice(width - tile, width)
    early = times(cross[:, :end], upper, final)
    rest = cross[:, end:] - early[:, LANE:]
    late = times(rest, lower, final)
    out_ref[:, width - tile : end] = early[:, :LANE] + late[:, :LANE]
    out_ref[:, end:] = late[:, LANE:]
    for start in range(0, width - tile, tile):
        columns = slice(start, start + tile)
        out_ref[:, columns] = times(cross[:, :end], upper, columns) + times(rest, lower, columns)


def solve(own, other, parts):
    return pl.pallas_call(
        solve_kernel,
        out_shape=jax.ShapeDtypeStruct(own.shape, jnp.float32),
        in_specs=[WHOLE] * 5,
        out_specs=WHOLE,
        compiler_params=ROOM,
        cost_estimate=pl.CostEstimate(
            flops=12 * own.size * own.shape[1], bytes_accessed=7 * 2**20, transcendentals=0
        ),
    )(own, other, *parts)


def partial_kernel(place_ref, codes_ref, activations_ref, own_ref, other_ref, gram_ref, gram_other_ref, strip_ref):
    core, z = place_ref[0], place_ref[1]
    width = own_ref.shape[0]
    blocks = codes_ref.shape[1] // LANE
    half = LANE // 2
    low = codes_ref[...].astype(jnp.bfloat16)
    for part_ref, index in ((other_ref, 1 - core), (own_ref, core)):
        channels = activations_ref[:, pl.ds(pl.multiple_of(index * width, width), width)]
        part_ref[...] = contract(channels, low)

    def strip(d):
        start = pl.multiple_of(lax.rem(z + d, blocks) * LANE, LANE)
        return [part.astype(jnp.bfloat16) for part in split(codes_ref[:, pl.ds(start, LANE)])]

    ours = strip(0)
    for d in range(STRIP):
        theirs = ours if d == 0 else strip(d)
        terms = [contract(ours[i], theirs[j]) for i, j in ((2, 0), (0, 2), (1, 1), (1, 0), (0, 1), (0, 0))]
        strip_ref[:, d * LANE : (d + 1) * LANE] = functools.reduce(jnp.add, terms)
    gram_ref[...] = strip_ref[pl.ds(pl.multiple_of(core * half, half), half), :]
    gram_other_ref[...] = strip_ref[pl.ds(pl.multiple_of((1 - core) * half, half), half), :]


def contract(left, right):
    return lax.dot_general(left, right, (((0,), (0,)), ((), ())), preferred_element_type=jnp.float32)


def partial_terms(place, codes, activations):
    width = activations.shape[1] // 2
    moments = jax.ShapeDtypeStruct((width, codes.shape[1]), jnp.float32)
    gram = jax.ShapeDtypeStruct((LANE // 2, STRIP * LANE), jnp.float32)
    return pl.pallas_call(
        partial_kernel,
        out_shape=(moments, moments, gram, gram),
        in_specs=[SCALARS, WHOLE, WHOLE],
        out_specs=(WHOLE,) * 4,
        scratch_shapes=[pltpu.VMEM((LANE, STRIP * LANE), jnp.float32)],
        compiler_params=ROOM,
        cost_estimate=pl.CostEstimate(
            flops=5 * 10**8, bytes_accessed=4 * 2**20, transcendentals=0
        ),
    )(place, codes, activations)


def cross_kernel(place_ref, weight_ref, part_ref, *refs):
    out_ref = refs[-1]
    width = part_ref.shape[0]
    rows = weight_ref.shape[0] // 16
    tile = 256
    core, y_hi = place_ref[0], place_ref[1]
    left = weight_ref[:, pl.ds(pl.multiple_of(core * width, width), width)]
    for n in range(out_ref.shape[1] // tile):
        columns = slice(n * tile, (n + 1) * tile)
        result = tree_sum(
            [product(left, part.astype(jnp.bfloat16)) for part in split(part_ref[:, columns])]
        )
        for y in range(2):
            offset = lax.rem(y + y_hi, 2) * rows
            for z in range(8):
                source = (y * 8 + z) * rows
                value = result[source : source + rows, :]
                target = pl.ds(pl.multiple_of(z * 2 * rows + offset, SUB), rows)
                for earlier in refs[:-1]:
                    value = value + earlier[target, columns]
                out_ref[target, columns] = value


def cross_terms(core, y_hi, weight, part, *earlier):
    place = jnp.stack([core, y_hi]).astype(jnp.int32)
    return pl.pallas_call(
        cross_kernel,
        out_shape=jax.ShapeDtypeStruct((weight.shape[0], part.shape[1]), jnp.float32),
        in_specs=[SCALARS] + [WHOLE] * (2 + len(earlier)),
        out_specs=WHOLE,
        compiler_params=ROOM,
        cost_estimate=pl.CostEstimate(
            flops=3 * weight.size * part.shape[1], bytes_accessed=8 * 2**20, transcendentals=0
        ),
    )(place, weight, part, *earlier)


def exchange_sum(value, axes, count):
    received = lax.all_to_all(value, axes, 0, 0, tiled=True)
    return received.reshape(count, -1, value.shape[1]).sum(0)


def exchange_gather(value, axes, count):
    copies = jnp.broadcast_to(value[None], (count,) + value.shape)
    return lax.all_to_all(copies.reshape(-1, value.shape[1]), axes, 0, 0, tiled=True)


def swap(value, axis):
    return lax.ppermute(value, axis, [(0, 1), (1, 0)])


def shards(activations, weight, basis):
    core, y_hi, z = (lax.axis_index(name) for name in ("core", "y_hi", "z"))
    partial_value = lax.dot_general(
        activations, basis, (((1,), (1,)), ((), ())), preferred_element_type=jnp.float32
    )
    codes = exchange_gather(exchange_sum(partial_value, CH, 16), CH, 16)

    here = core.astype(jnp.int32)[None]
    place = jnp.stack([core, z]).astype(jnp.int32)
    own, other, gram, gram_other = partial_terms(place, codes, activations)
    gram = gram + swap(gram_other, "core")
    own = own + swap(other, "core")
    gram = exchange_gather(exchange_sum(gram, PLANE, 8), PLANE, 8)
    gram = jnp.concatenate([gram, gram], 1)
    own, gram = lax.optimization_barrier((own, gram))
    gram = lax.all_gather(gram, "z", axis=0, tiled=True)
    own = exchange_gather(exchange_sum(own, PLANE, 8), PLANE, 8)
    cross = cross_terms(core, y_hi, weight, own)
    cross = cross_terms(1 - core, y_hi, weight, swap(own, "core"), cross)
    cross, gram = lax.optimization_barrier((cross, gram))
    cross = lax.psum_scatter(cross, "z", scatter_dimension=0, tiled=True)
    gram = gram[:, : STRIP * LANE]
    inverse = swept(here, gram, swap(gram, "core"))
    cross, inverse = lax.optimization_barrier((cross, inverse))
    half = cross.shape[0] // 2
    return solve(cross[:half], swap(cross[half:], "y_hi"), split_rows(inverse))


def solution(mesh):
    names = tuple(name for name, _ in AXES)
    fine = Mesh(mesh.devices.reshape([size for _, size in AXES]), names)
    in_specs = (P(TOK, CH), P(TOK, CH), P(None, CH))
    out_specs = P(TOK + CH, None)
    return jax.shard_map(shards, mesh=fine, in_specs=in_specs, out_specs=out_specs, check_vma=False)
```

```python
import functools

import jax
import jax.numpy as jnp
from jax import lax
from jax.experimental import pallas as pl
from jax.experimental.pallas import tpu as pltpu
from jax.sharding import Mesh
from jax.sharding import PartitionSpec as P

damping = 0.1

SUB, LANE = 8, 128
STRIP = 5
AXES = (("x", 4), ("y_lo", 2), ("core", 2), ("y_hi", 2), ("z", 8))
TOK = ("x", "y_lo", "core")
PLANE = ("x", "y_lo")
CH = ("y_hi", "z")


def tree_sum(terms):
    while len(terms) > 1:
        paired = [a + b for a, b in zip(terms[::2], terms[1::2])]
        terms = paired + ([terms[-1]] if len(terms) % 2 else [])
    return terms[0]


def spread(value):
    return jnp.broadcast_to(value, (SUB, LANE))


def invert_small(entry):
    for k in range(SUB):
        inverse = 1.0 / entry[k, k]
        row = [entry[min(k, j), max(k, j)] for j in range(SUB)]
        scaled = [value * inverse for value in row]
        for i in range(SUB):
            for j in range(i, SUB):
                if i != k and j != k:
                    entry[i, j] = entry[i, j] - scaled[i] * row[j]
        for j in range(SUB):
            if j != k:
                entry[min(k, j), max(k, j)] = scaled[j]
        entry[k, k] = -inverse
    return {place: -value for place, value in entry.items()}


def combine(columns, rows):
    return tree_sum([column * row for column, row in zip(columns, rows)])


def pick(sub, values):
    pairs = [jnp.where(sub == i, values[i], values[i + 1]) for i in range(0, SUB, 2)]
    low, high = jnp.where(sub < 2, *pairs[:2]), jnp.where(sub < 6, *pairs[2:])
    return jnp.where(sub < 4, low, high)


def invert_block(block, buffer, between=None):
    sub = lax.broadcasted_iota(jnp.int32, (SUB, LANE), 0)
    lane = lax.broadcasted_iota(jnp.int32, (SUB, LANE), 1)
    panels = LANE // SUB
    rows = [block[r * SUB : (r + 1) * SUB, :] for r in range(panels)]
    for p in range(panels):
        base = p * SUB
        panel = rows[p]
        inside = (lane >= base) & (lane < base + SUB)
        offset = (p % 2) * (SUB + 2) * SUB

        def rows_of(slot, value):
            start = offset + slot * SUB
            buffer[start : start + SUB, :] = value
            return [spread(buffer[start + i : start + i + 1, :]) for i in range(SUB)]

        def columns_of(value):
            return [spread(value[:, base + j : base + j + 1]) for j in range(SUB)]

        entries = [rows_of(j, column) for j, column in enumerate(columns_of(panel))]
        small = invert_small({(i, j): entries[j][i] for j in range(SUB) for i in range(j + 1)})
        small_columns = [
            pick(sub, [small[min(i, j), max(i, j)] for i in range(SUB)]) for j in range(SUB)
        ]
        wide = jnp.where(inside, jnp.where(lane - base == sub, 1.0, 0.0), panel)
        pivot = combine(small_columns, rows_of(SUB, wide))
        left = jnp.concatenate(left_list(jnp.where(lane < base, -panel, panel)), 0)
        right = jnp.concatenate(right_list(pivot), 0)
        change = lax.dot_general(
            left.astype(jnp.bfloat16),
            right.astype(jnp.bfloat16),
            (((0,), (0,)), ((), ())),
            preferred_element_type=jnp.float32,
        )
        for r in range(panels):
            if r == p + 1:
                amount = combine(columns_of(rows[r]), rows_of(SUB + 1, pivot))
            else:
                amount = change[r * SUB : (r + 1) * SUB, :]
            if r != p:
                rows[r] = jnp.where(inside, 0.0, rows[r]) - amount
        rows[p] = pivot
        if between is not None:
            between(p)
    return rows


def split(value):
    high = value.astype(jnp.bfloat16).astype(jnp.float32)
    rest = value - high
    middle = rest.astype(jnp.bfloat16).astype(jnp.float32)
    return high, middle, rest - middle


def left_list(value):
    high, middle, low = split(value)
    return [high, middle, high, middle, high, low]


def right_list(value):
    high, middle, low = split(value)
    return [high, high, middle, middle, low, high]


def left_parts(value):
    return jnp.concatenate([part.astype(jnp.bfloat16) for part in left_list(value)], 1)


def right_parts(value):
    return jnp.concatenate([part.astype(jnp.bfloat16) for part in right_list(value)], 0)


def product(left, right):
    return jnp.dot(left, right, preferred_element_type=jnp.float32)


def inverse_kernel(
    place_ref, own_ref, other_ref, result_ref, out_ref, left_ref, right_ref, block_ref, buffer, done
):
    size = out_ref.shape[0]
    blocks = size // LANE
    tile = 256
    half = LANE // 2
    core = place_ref[0]
    row = lax.broadcasted_iota(jnp.int32, (LANE, LANE), 0)
    column = lax.broadcasted_iota(jnp.int32, (LANE, LANE), 1)
    diagonal = row == column
    for a in range(blocks):
        for d in range(STRIP):
            b = (a + d) % blocks
            place, source = slice(b * LANE, (b + 1) * LANE), slice(d * LANE, (d + 1) * LANE)
            for part_ref, index in ((own_ref, core), (other_ref, 1 - core)):
                rows = pl.ds(pl.multiple_of(a * LANE + index * half, half), half)
                out_ref[rows, place] = part_ref[a * half : (a + 1) * half, source]
    total = jnp.zeros((LANE, LANE), jnp.float32)
    for a in range(blocks):
        ours = slice(a * LANE, (a + 1) * LANE)
        total = total + jnp.where(diagonal, out_ref[ours, ours], 0.0)
        for d in range(1, blocks // 2):
            b = (a + d) % blocks
            theirs = slice(b * LANE, (b + 1) * LANE)
            out_ref[theirs, ours] = out_ref[ours, theirs].T
    ridge = damping * jnp.sum(total) / size
    for a in range(blocks):
        ours = slice(a * LANE, (a + 1) * LANE)
        out_ref[ours, ours] = out_ref[ours, ours] + jnp.where(diagonal, ridge, 0.0)

    def keep(rows):
        for r in range(LANE // SUB):
            block_ref[r * SUB : (r + 1) * SUB, :] = rows[r]

    keep(invert_block(out_ref[0:LANE, 0:LANE], buffer))

    def pivot_rows(here, inverse):
        inverse_parts = left_parts(inverse)
        for m in range(size // tile):
            columns = slice(m * tile, (m + 1) * tile)
            scaled = product(inverse_parts, right_parts(out_ref[here, columns]))
            right_ref[:, columns] = right_parts(scaled)
            out_ref[here, columns] = scaled

    def step(k, carry):
        here = pl.ds(pl.multiple_of(k * LANE, LANE), LANE)
        after = pl.ds(pl.multiple_of((k + 1) * LANE, LANE), LANE)
        inverse = block_ref[...]
        ahead = product(left_parts(inverse), right_parts(out_ref[here, after]))
        following = out_ref[after, after] - product(
            left_parts(out_ref[after, here]), right_parts(ahead)
        )
        for m in range(blocks):
            rows = slice(m * LANE, (m + 1) * LANE)
            left_ref[rows, :] = left_parts(out_ref[rows, here])
        left_ref[here, :] = jnp.zeros((LANE, 6 * LANE), jnp.bfloat16)
        pivot_rows(here, inverse)
        out_ref[:, here] = jnp.zeros((size, LANE), jnp.float32)
        out_ref[here, here] = inverse
        right_ref[:, here] = right_parts(inverse)

        def update(p):
            m, n = divmod(p, size // tile)
            columns = slice(n * tile, (n + 1) * tile)
            rows = slice(m * tile, (m + 1) * tile)
            out_ref[rows, columns] = out_ref[rows, columns] - product(
                left_ref[rows, :], right_ref[:, columns]
            )

        keep(invert_block(following, buffer, update))
        return carry

    lax.fori_loop(0, blocks - 1, step, 0)
    end = size - LANE
    upper = pltpu.make_async_copy(out_ref.at[:end], result_ref.at[:end], done.at[0])
    upper.start()
    inverse = block_ref[...]
    pivot_rows(slice(end, size), inverse)
    out_ref[end:, end:] = inverse
    lower = pltpu.make_async_copy(out_ref.at[end:], result_ref.at[end:], done.at[1])
    lower.start()
    upper.wait()
    lower.wait()


WHOLE = pl.BlockSpec(memory_space=pltpu.VMEM)
OUTSIDE = pl.BlockSpec(memory_space=pltpu.HBM)
SCALARS = pl.BlockSpec(memory_space=pltpu.SMEM)
ROOM = pltpu.CompilerParams(vmem_limit_bytes=40 * 2**20)
MOST = pltpu.CompilerParams(vmem_limit_bytes=58 * 2**20)


def swept(place, own, other):
    size = 2 * own.shape[0]
    return pl.pallas_call(
        inverse_kernel,
        out_shape=jax.ShapeDtypeStruct((size, size), jnp.float32),
        in_specs=[SCALARS, WHOLE, WHOLE],
        out_specs=OUTSIDE,
        scratch_shapes=[
            pltpu.VMEM((size, size), jnp.float32),
            pltpu.VMEM((size, 6 * LANE), jnp.bfloat16),
            pltpu.VMEM((6 * LANE, size), jnp.bfloat16),
            pltpu.VMEM((LANE, LANE), jnp.float32),
            pltpu.VMEM((2 * (SUB + 2) * SUB, LANE), jnp.float32),
            pltpu.SemaphoreType.DMA((2,)),
        ],
        compiler_params=MOST,
        cost_estimate=pl.CostEstimate(
            flops=12 * size**3, bytes_accessed=8 * size**2, transcendentals=0
        ),
    )(place, own, other)


def split_kernel(value_ref, high_ref, middle_ref, low_ref):
    for part_ref, part in zip((high_ref, middle_ref, low_ref), split(value_ref[...])):
        part_ref[...] = part.astype(jnp.bfloat16)


def split_rows(value):
    rows, width = value.shape
    tile = 128
    spec = pl.BlockSpec((tile, width), lambda n: (n, 0))
    part = jax.ShapeDtypeStruct(value.shape, jnp.bfloat16)
    return pl.pallas_call(
        split_kernel,
        grid=(rows // tile,),
        out_shape=(part,) * 3,
        in_specs=[spec],
        out_specs=(spec,) * 3,
        compiler_params=ROOM,
        cost_estimate=pl.CostEstimate(
            flops=8 * value.size, bytes_accessed=10 * value.size, transcendentals=0
        ),
    )(value)


def solve_kernel(own_ref, other_ref, high_ref, middle_ref, low_ref, out_ref):
    rows, width = out_ref.shape
    end = width - LANE

    def times(value, span, columns):
        left = [part.astype(jnp.bfloat16) for part in split(value)]
        by_high = product(jnp.concatenate(left, 0), high_ref[span, columns])
        by_middle = product(jnp.concatenate(left[:2], 0), middle_ref[span, columns])
        small = by_middle[rows:] + by_high[2 * rows :] + product(left[0], low_ref[span, columns])
        return by_high[:rows] + (by_high[rows : 2 * rows] + by_middle[:rows] + small)

    cross = own_ref[...] + other_ref[...]
    tile = 2 * LANE
    upper, lower = slice(0, end), slice(end, width)
    final = slice(width - tile, width)
    early = times(cross[:, :end], upper, final)
    rest = cross[:, end:] - early[:, LANE:]
    late = times(rest, lower, final)
    out_ref[:, width - tile : end] = early[:, :LANE] + late[:, :LANE]
    out_ref[:, end:] = late[:, LANE:]
    for start in range(0, width - tile, tile):
        columns = slice(start, start + tile)
        out_ref[:, columns] = times(cross[:, :end], upper, columns) + times(rest, lower, columns)


def solve(own, other, parts):
    return pl.pallas_call(
        solve_kernel,
        out_shape=jax.ShapeDtypeStruct(own.shape, jnp.float32),
        in_specs=[WHOLE] * 5,
        out_specs=WHOLE,
        compiler_params=ROOM,
        cost_estimate=pl.CostEstimate(
            flops=12 * own.size * own.shape[1], bytes_accessed=7 * 2**20, transcendentals=0
        ),
    )(own, other, *parts)


def partial_kernel(place_ref, codes_ref, activations_ref, own_ref, other_ref, gram_ref, gram_other_ref, strip_ref):
    core, z = place_ref[0], place_ref[1]
    width = own_ref.shape[0]
    blocks = codes_ref.shape[1] // LANE
    half = LANE // 2
    low = codes_ref[...].astype(jnp.bfloat16)
    for part_ref, index in ((other_ref, 1 - core), (own_ref, core)):
        channels = activations_ref[:, pl.ds(pl.multiple_of(index * width, width), width)]
        part_ref[...] = contract(channels, low)

    def strip(d):
        start = pl.multiple_of(lax.rem(z + d, blocks) * LANE, LANE)
        return [part.astype(jnp.bfloat16) for part in split(codes_ref[:, pl.ds(start, LANE)])]

    ours = strip(0)
    for d in range(STRIP):
        theirs = ours if d == 0 else strip(d)
        terms = [contract(ours[i], theirs[j]) for i, j in ((2, 0), (0, 2), (1, 1), (1, 0), (0, 1), (0, 0))]
        strip_ref[:, d * LANE : (d + 1) * LANE] = functools.reduce(jnp.add, terms)
    gram_ref[...] = strip_ref[pl.ds(pl.multiple_of(core * half, half), half), :]
    gram_other_ref[...] = strip_ref[pl.ds(pl.multiple_of((1 - core) * half, half), half), :]


def contract(left, right):
    return lax.dot_general(left, right, (((0,), (0,)), ((), ())), preferred_element_type=jnp.float32)


def partial_terms(place, codes, activations):
    width = activations.shape[1] // 2
    moments = jax.ShapeDtypeStruct((width, codes.shape[1]), jnp.float32)
    gram = jax.ShapeDtypeStruct((LANE // 2, STRIP * LANE), jnp.float32)
    return pl.pallas_call(
        partial_kernel,
        out_shape=(moments, moments, gram, gram),
        in_specs=[SCALARS, WHOLE, WHOLE],
        out_specs=(WHOLE,) * 4,
        scratch_shapes=[pltpu.VMEM((LANE, STRIP * LANE), jnp.float32)],
        compiler_params=ROOM,
        cost_estimate=pl.CostEstimate(
            flops=5 * 10**8, bytes_accessed=4 * 2**20, transcendentals=0
        ),
    )(place, codes, activations)


def cross_kernel(place_ref, weight_ref, part_ref, *refs):
    out_ref = refs[-1]
    width = part_ref.shape[0]
    rows = weight_ref.shape[0] // 16
    tile = 256
    core, y_hi = place_ref[0], place_ref[1]
    left = weight_ref[:, pl.ds(pl.multiple_of(core * width, width), width)]
    for n in range(out_ref.shape[1] // tile):
        columns = slice(n * tile, (n + 1) * tile)
        result = tree_sum(
            [product(left, part.astype(jnp.bfloat16)) for part in split(part_ref[:, columns])]
        )
        for y in range(2):
            offset = lax.rem(y + y_hi, 2) * rows
            for z in range(8):
                source = (y * 8 + z) * rows
                value = result[source : source + rows, :]
                target = pl.ds(pl.multiple_of(z * 2 * rows + offset, SUB), rows)
                for earlier in refs[:-1]:
                    value = value + earlier[target, columns]
                out_ref[target, columns] = value


def cross_terms(place, weight, part, *earlier):
    return pl.pallas_call(
        cross_kernel,
        out_shape=jax.ShapeDtypeStruct((weight.shape[0], part.shape[1]), jnp.float32),
        in_specs=[SCALARS] + [WHOLE] * (2 + len(earlier)),
        out_specs=WHOLE,
        compiler_params=ROOM,
        cost_estimate=pl.CostEstimate(
            flops=3 * weight.size * part.shape[1], bytes_accessed=8 * 2**20, transcendentals=0
        ),
    )(place, weight, part, *earlier)


def exchange_sum(value, axes, count):
    received = lax.all_to_all(value, axes, 0, 0, tiled=True)
    return received.reshape(count, -1, value.shape[1]).sum(0)


def exchange_gather(value, axes, count):
    copies = jnp.broadcast_to(value[None], (count,) + value.shape)
    return lax.all_to_all(copies.reshape(-1, value.shape[1]), axes, 0, 0, tiled=True)


def swap(value, axis):
    return lax.ppermute(value, axis, [(0, 1), (1, 0)])


def shards(activations, weight, basis):
    core, y_hi, z = (lax.axis_index(name).astype(jnp.int32) for name in ("core", "y_hi", "z"))
    activations, core, y_hi, z = lax.optimization_barrier((activations, core, y_hi, z))
    partial_value = lax.dot_general(
        activations, basis, (((1,), (1,)), ((), ())), preferred_element_type=jnp.float32
    )
    codes = exchange_gather(exchange_sum(partial_value, CH, 16), CH, 16)
    codes, core, y_hi, z = lax.optimization_barrier((codes, core, y_hi, z))
    place = jnp.stack([core, z])
    places = [jnp.stack([index, y_hi]) for index in (core, 1 - core)]

    own, other, gram, gram_other = partial_terms(place, codes, activations)
    gram = gram + swap(gram_other, "core")
    other = swap(other, "core")
    gram = exchange_gather(exchange_sum(gram, PLANE, 8), PLANE, 8)
    gram = jnp.concatenate([gram, gram], 1)
    other, gram = lax.optimization_barrier((other, gram))
    own = own + other
    gram = lax.all_gather(gram, "z", axis=0, tiled=True)
    own = exchange_gather(exchange_sum(own, PLANE, 8), PLANE, 8)
    cross = cross_terms(places[0], weight, own)
    cross = cross_terms(places[1], weight, swap(own, "core"), cross)
    cross, gram = lax.optimization_barrier((cross, gram))
    cross = lax.psum_scatter(cross, "z", scatter_dimension=0, tiled=True)
    gram = gram[:, : STRIP * LANE]
    inverse = swept(place, gram, swap(gram, "core"))
    cross, inverse = lax.optimization_barrier((cross, inverse))
    half = cross.shape[0] // 2
    return solve(cross[:half], swap(cross[half:], "y_hi"), split_rows(inverse))


def solution(mesh):
    names = tuple(name for name, _ in AXES)
    fine = Mesh(mesh.devices.reshape([size for _, size in AXES]), names)
    in_specs = (P(TOK, CH), P(TOK, CH), P(None, CH))
    out_specs = P(TOK + CH, None)
    return jax.shard_map(shards, mesh=fine, in_specs=in_specs, out_specs=out_specs, check_vma=False)
```

```python
import functools

import jax
import jax.numpy as jnp
from jax import lax
from jax.experimental import pallas as pl
from jax.experimental.pallas import tpu as pltpu
from jax.sharding import Mesh
from jax.sharding import PartitionSpec as P

damping = 0.1

SUB, LANE = 8, 128
STRIP = 5
AXES = (("x", 4), ("y_lo", 2), ("core", 2), ("y_hi", 2), ("z", 8))
TOK = ("x", "y_lo", "core")
PLANE = ("x", "y_lo")
CH = ("y_hi", "z")


def tree_sum(terms):
    while len(terms) > 1:
        paired = [a + b for a, b in zip(terms[::2], terms[1::2])]
        terms = paired + ([terms[-1]] if len(terms) % 2 else [])
    return terms[0]


def spread(value):
    return jnp.broadcast_to(value, (SUB, LANE))


def invert_small(entry):
    for k in range(SUB):
        inverse = 1.0 / entry[k, k]
        row = [entry[min(k, j), max(k, j)] for j in range(SUB)]
        scaled = [value * inverse for value in row]
        for i in range(SUB):
            for j in range(i, SUB):
                if i != k and j != k:
                    entry[i, j] = entry[i, j] - scaled[i] * row[j]
        for j in range(SUB):
            if j != k:
                entry[min(k, j), max(k, j)] = scaled[j]
        entry[k, k] = -inverse
    return {place: -value for place, value in entry.items()}


def combine(columns, rows):
    return tree_sum([column * row for column, row in zip(columns, rows)])


def pick(sub, values):
    pairs = [jnp.where(sub == i, values[i], values[i + 1]) for i in range(0, SUB, 2)]
    low, high = jnp.where(sub < 2, *pairs[:2]), jnp.where(sub < 6, *pairs[2:])
    return jnp.where(sub < 4, low, high)


def invert_block(block, buffer, between=None):
    sub = lax.broadcasted_iota(jnp.int32, (SUB, LANE), 0)
    lane = lax.broadcasted_iota(jnp.int32, (SUB, LANE), 1)
    panels = LANE // SUB
    rows = [block[r * SUB : (r + 1) * SUB, :] for r in range(panels)]
    for p in range(panels):
        base = p * SUB
        panel = rows[p]
        inside = (lane >= base) & (lane < base + SUB)
        offset = (p % 2) * (SUB + 2) * SUB

        def rows_of(slot, value):
            start = offset + slot * SUB
            buffer[start : start + SUB, :] = value
            return [spread(buffer[start + i : start + i + 1, :]) for i in range(SUB)]

        def columns_of(value):
            return [spread(value[:, base + j : base + j + 1]) for j in range(SUB)]

        entries = [rows_of(j, column) for j, column in enumerate(columns_of(panel))]
        small = invert_small({(i, j): entries[j][i] for j in range(SUB) for i in range(j + 1)})
        small_columns = [
            pick(sub, [small[min(i, j), max(i, j)] for i in range(SUB)]) for j in range(SUB)
        ]
        wide = jnp.where(inside, jnp.where(lane - base == sub, 1.0, 0.0), panel)
        pivot = combine(small_columns, rows_of(SUB, wide))
        left = jnp.concatenate(left_list(jnp.where(lane < base, -panel, panel)), 0)
        right = jnp.concatenate(right_list(pivot), 0)
        change = lax.dot_general(
            left.astype(jnp.bfloat16),
            right.astype(jnp.bfloat16),
            (((0,), (0,)), ((), ())),
            preferred_element_type=jnp.float32,
        )
        for r in range(panels):
            if r == p + 1:
                amount = combine(columns_of(rows[r]), rows_of(SUB + 1, pivot))
            else:
                amount = change[r * SUB : (r + 1) * SUB, :]
            if r != p:
                rows[r] = jnp.where(inside, 0.0, rows[r]) - amount
        rows[p] = pivot
        if between is not None:
            between(p)
    return rows


def split(value):
    high = value.astype(jnp.bfloat16).astype(jnp.float32)
    rest = value - high
    middle = rest.astype(jnp.bfloat16).astype(jnp.float32)
    return high, middle, rest - middle


def left_list(value):
    high, middle, low = split(value)
    return [high, middle, high, middle, high, low]


def right_list(value):
    high, middle, low = split(value)
    return [high, high, middle, middle, low, high]


def left_parts(value):
    return jnp.concatenate([part.astype(jnp.bfloat16) for part in left_list(value)], 1)


def right_parts(value):
    return jnp.concatenate([part.astype(jnp.bfloat16) for part in right_list(value)], 0)


def product(left, right):
    return jnp.dot(left, right, preferred_element_type=jnp.float32)


def inverse_kernel(
    place_ref, own_ref, other_ref, result_ref, out_ref, left_ref, right_ref, block_ref, buffer, done
):
    size = out_ref.shape[0]
    blocks = size // LANE
    tile = 256
    half = LANE // 2
    core = place_ref[0]
    row = lax.broadcasted_iota(jnp.int32, (LANE, LANE), 0)
    column = lax.broadcasted_iota(jnp.int32, (LANE, LANE), 1)
    diagonal = row == column
    for a in range(blocks):
        for d in range(STRIP):
            b = (a + d) % blocks
            place, source = slice(b * LANE, (b + 1) * LANE), slice(d * LANE, (d + 1) * LANE)
            for part_ref, index in ((own_ref, core), (other_ref, 1 - core)):
                rows = pl.ds(pl.multiple_of(a * LANE + index * half, half), half)
                out_ref[rows, place] = part_ref[a * half : (a + 1) * half, source]
    total = jnp.zeros((LANE, LANE), jnp.float32)
    for a in range(blocks):
        ours = slice(a * LANE, (a + 1) * LANE)
        total = total + jnp.where(diagonal, out_ref[ours, ours], 0.0)
        for d in range(1, blocks // 2):
            b = (a + d) % blocks
            theirs = slice(b * LANE, (b + 1) * LANE)
            out_ref[theirs, ours] = out_ref[ours, theirs].T
    ridge = damping * jnp.sum(total) / size
    for a in range(blocks):
        ours = slice(a * LANE, (a + 1) * LANE)
        out_ref[ours, ours] = out_ref[ours, ours] + jnp.where(diagonal, ridge, 0.0)

    def keep(rows):
        for r in range(LANE // SUB):
            block_ref[r * SUB : (r + 1) * SUB, :] = rows[r]

    keep(invert_block(out_ref[0:LANE, 0:LANE], buffer))

    def pivot_rows(here, inverse):
        inverse_parts = left_parts(inverse)
        for m in range(size // tile):
            columns = slice(m * tile, (m + 1) * tile)
            scaled = product(inverse_parts, right_parts(out_ref[here, columns]))
            right_ref[:, columns] = right_parts(scaled)
            out_ref[here, columns] = scaled

    end = size - LANE
    copies = []

    def send(rows):
        copy = pltpu.make_async_copy(out_ref.at[rows], result_ref.at[rows], done.at[len(copies)])
        copy.start()
        copies.append(copy)

    def step(k, last):
        here = pl.ds(pl.multiple_of(k * LANE, LANE), LANE)
        after = pl.ds(pl.multiple_of((k + 1) * LANE, LANE), LANE)
        inverse = block_ref[...]
        ahead = product(left_parts(inverse), right_parts(out_ref[here, after]))
        following = out_ref[after, after] - product(
            left_parts(out_ref[after, here]), right_parts(ahead)
        )
        for m in range(blocks):
            rows = slice(m * LANE, (m + 1) * LANE)
            left_ref[rows, :] = left_parts(out_ref[rows, here])
        left_ref[here, :] = jnp.zeros((LANE, 6 * LANE), jnp.bfloat16)
        pivot_rows(here, inverse)
        out_ref[:, here] = jnp.zeros((size, LANE), jnp.float32)
        out_ref[here, here] = inverse
        right_ref[:, here] = right_parts(inverse)

        def update(p):
            m, n = divmod(p, size // tile)
            columns = slice(n * tile, (n + 1) * tile)
            rows = slice(m * tile, (m + 1) * tile)
            out_ref[rows, columns] = out_ref[rows, columns] - product(
                left_ref[rows, :], right_ref[:, columns]
            )
            if last and n == size // tile - 1:
                send(slice(m * tile, min((m + 1) * tile, end)))

        keep(invert_block(following, buffer, update))

    def early_step(k, carry):
        step(k, False)
        return carry

    lax.fori_loop(0, blocks - 2, early_step, 0)
    step(blocks - 2, True)
    inverse = block_ref[...]
    pivot_rows(slice(end, size), inverse)
    out_ref[end:, end:] = inverse
    send(slice(end, size))
    for copy in copies:
        copy.wait()


WHOLE = pl.BlockSpec(memory_space=pltpu.VMEM)
OUTSIDE = pl.BlockSpec(memory_space=pltpu.HBM)
SCALARS = pl.BlockSpec(memory_space=pltpu.SMEM)
ROOM = pltpu.CompilerParams(vmem_limit_bytes=40 * 2**20)
MOST = pltpu.CompilerParams(vmem_limit_bytes=58 * 2**20)


def swept(place, own, other):
    size = 2 * own.shape[0]
    return pl.pallas_call(
        inverse_kernel,
        out_shape=jax.ShapeDtypeStruct((size, size), jnp.float32),
        in_specs=[SCALARS, WHOLE, WHOLE],
        out_specs=OUTSIDE,
        scratch_shapes=[
            pltpu.VMEM((size, size), jnp.float32),
            pltpu.VMEM((size, 6 * LANE), jnp.bfloat16),
            pltpu.VMEM((6 * LANE, size), jnp.bfloat16),
            pltpu.VMEM((LANE, LANE), jnp.float32),
            pltpu.VMEM((2 * (SUB + 2) * SUB, LANE), jnp.float32),
            pltpu.SemaphoreType.DMA((5,)),
        ],
        compiler_params=MOST,
        cost_estimate=pl.CostEstimate(
            flops=12 * size**3, bytes_accessed=8 * size**2, transcendentals=0
        ),
    )(place, own, other)


def split_kernel(value_ref, high_ref, middle_ref, low_ref):
    for part_ref, part in zip((high_ref, middle_ref, low_ref), split(value_ref[...])):
        part_ref[...] = part.astype(jnp.bfloat16)


def split_rows(value):
    rows, width = value.shape
    tile = 128
    spec = pl.BlockSpec((tile, width), lambda n: (n, 0))
    part = jax.ShapeDtypeStruct(value.shape, jnp.bfloat16)
    return pl.pallas_call(
        split_kernel,
        grid=(rows // tile,),
        out_shape=(part,) * 3,
        in_specs=[spec],
        out_specs=(spec,) * 3,
        compiler_params=ROOM,
        cost_estimate=pl.CostEstimate(
            flops=8 * value.size, bytes_accessed=10 * value.size, transcendentals=0
        ),
    )(value)


def solve_kernel(own_ref, other_ref, high_ref, middle_ref, low_ref, out_ref):
    rows, width = out_ref.shape
    end = width - LANE

    def times(value, span, columns):
        left = [part.astype(jnp.bfloat16) for part in split(value)]
        by_high = product(jnp.concatenate(left, 0), high_ref[span, columns])
        by_middle = product(jnp.concatenate(left[:2], 0), middle_ref[span, columns])
        small = by_middle[rows:] + by_high[2 * rows :] + product(left[0], low_ref[span, columns])
        return by_high[:rows] + (by_high[rows : 2 * rows] + by_middle[:rows] + small)

    cross = own_ref[...] + other_ref[...]
    tile = 2 * LANE
    upper, lower = slice(0, end), slice(end, width)
    final = slice(width - tile, width)
    early = times(cross[:, :end], upper, final)
    rest = cross[:, end:] - early[:, LANE:]
    late = times(rest, lower, final)
    out_ref[:, width - tile : end] = early[:, :LANE] + late[:, :LANE]
    out_ref[:, end:] = late[:, LANE:]
    for start in range(0, width - tile, tile):
        columns = slice(start, start + tile)
        out_ref[:, columns] = times(cross[:, :end], upper, columns) + times(rest, lower, columns)


def solve(own, other, parts):
    return pl.pallas_call(
        solve_kernel,
        out_shape=jax.ShapeDtypeStruct(own.shape, jnp.float32),
        in_specs=[WHOLE] * 5,
        out_specs=WHOLE,
        compiler_params=ROOM,
        cost_estimate=pl.CostEstimate(
            flops=12 * own.size * own.shape[1], bytes_accessed=7 * 2**20, transcendentals=0
        ),
    )(own, other, *parts)


def partial_kernel(place_ref, codes_ref, activations_ref, own_ref, other_ref, gram_ref, gram_other_ref, strip_ref):
    core, z = place_ref[0], place_ref[1]
    width = own_ref.shape[0]
    blocks = codes_ref.shape[1] // LANE
    half = LANE // 2
    low = codes_ref[...].astype(jnp.bfloat16)
    for part_ref, index in ((other_ref, 1 - core), (own_ref, core)):
        channels = activations_ref[:, pl.ds(pl.multiple_of(index * width, width), width)]
        part_ref[...] = contract(channels, low)

    def strip(d):
        start = pl.multiple_of(lax.rem(z + d, blocks) * LANE, LANE)
        return [part.astype(jnp.bfloat16) for part in split(codes_ref[:, pl.ds(start, LANE)])]

    ours = strip(0)
    for d in range(STRIP):
        theirs = ours if d == 0 else strip(d)
        terms = [contract(ours[i], theirs[j]) for i, j in ((2, 0), (0, 2), (1, 1), (1, 0), (0, 1), (0, 0))]
        strip_ref[:, d * LANE : (d + 1) * LANE] = functools.reduce(jnp.add, terms)
    gram_ref[...] = strip_ref[pl.ds(pl.multiple_of(core * half, half), half), :]
    gram_other_ref[...] = strip_ref[pl.ds(pl.multiple_of((1 - core) * half, half), half), :]


def contract(left, right):
    return lax.dot_general(left, right, (((0,), (0,)), ((), ())), preferred_element_type=jnp.float32)


def partial_terms(place, codes, activations):
    width = activations.shape[1] // 2
    moments = jax.ShapeDtypeStruct((width, codes.shape[1]), jnp.float32)
    gram = jax.ShapeDtypeStruct((LANE // 2, STRIP * LANE), jnp.float32)
    return pl.pallas_call(
        partial_kernel,
        out_shape=(moments, moments, gram, gram),
        in_specs=[SCALARS, WHOLE, WHOLE],
        out_specs=(WHOLE,) * 4,
        scratch_shapes=[pltpu.VMEM((LANE, STRIP * LANE), jnp.float32)],
        compiler_params=ROOM,
        cost_estimate=pl.CostEstimate(
            flops=5 * 10**8, bytes_accessed=4 * 2**20, transcendentals=0
        ),
    )(place, codes, activations)


def cross_kernel(place_ref, weight_ref, part_ref, *refs):
    out_ref = refs[-1]
    width = part_ref.shape[0]
    rows = weight_ref.shape[0] // 16
    tile = 256
    core, y_hi = place_ref[0], place_ref[1]
    left = weight_ref[:, pl.ds(pl.multiple_of(core * width, width), width)]
    for n in range(out_ref.shape[1] // tile):
        columns = slice(n * tile, (n + 1) * tile)
        result = tree_sum(
            [product(left, part.astype(jnp.bfloat16)) for part in split(part_ref[:, columns])]
        )
        for y in range(2):
            offset = lax.rem(y + y_hi, 2) * rows
            for z in range(8):
                source = (y * 8 + z) * rows
                value = result[source : source + rows, :]
                target = pl.ds(pl.multiple_of(z * 2 * rows + offset, SUB), rows)
                for earlier in refs[:-1]:
                    value = value + earlier[target, columns]
                out_ref[target, columns] = value


def cross_terms(place, weight, part, *earlier):
    return pl.pallas_call(
        cross_kernel,
        out_shape=jax.ShapeDtypeStruct((weight.shape[0], part.shape[1]), jnp.float32),
        in_specs=[SCALARS] + [WHOLE] * (2 + len(earlier)),
        out_specs=WHOLE,
        compiler_params=ROOM,
        cost_estimate=pl.CostEstimate(
            flops=3 * weight.size * part.shape[1], bytes_accessed=8 * 2**20, transcendentals=0
        ),
    )(place, weight, part, *earlier)


def exchange_sum(value, axes, count):
    received = lax.all_to_all(value, axes, 0, 0, tiled=True)
    return received.reshape(count, -1, value.shape[1]).sum(0)


def exchange_gather(value, axes, count):
    copies = jnp.broadcast_to(value[None], (count,) + value.shape)
    return lax.all_to_all(copies.reshape(-1, value.shape[1]), axes, 0, 0, tiled=True)


def swap(value, axis):
    return lax.ppermute(value, axis, [(0, 1), (1, 0)])


def shards(activations, weight, basis):
    core, y_hi, z = (lax.axis_index(name).astype(jnp.int32) for name in ("core", "y_hi", "z"))
    activations, core, y_hi, z = lax.optimization_barrier((activations, core, y_hi, z))
    partial_value = lax.dot_general(
        activations, basis, (((1,), (1,)), ((), ())), preferred_element_type=jnp.float32
    )
    codes = exchange_gather(exchange_sum(partial_value, CH, 16), CH, 16)
    codes, core, y_hi, z = lax.optimization_barrier((codes, core, y_hi, z))
    place = jnp.stack([core, z])
    places = [jnp.stack([index, y_hi]) for index in (core, 1 - core)]

    own, other, gram, gram_other = partial_terms(place, codes, activations)
    gram = gram + swap(gram_other, "core")
    other = swap(other, "core")
    gram = exchange_gather(exchange_sum(gram, PLANE, 8), PLANE, 8)
    gram = jnp.concatenate([gram, gram], 1)
    other, gram = lax.optimization_barrier((other, gram))
    own = own + other
    gram = lax.all_gather(gram, "z", axis=0, tiled=True)
    own = exchange_gather(exchange_sum(own, PLANE, 8), PLANE, 8)
    cross = cross_terms(places[0], weight, own)
    cross = cross_terms(places[1], weight, swap(own, "core"), cross)
    cross, gram = lax.optimization_barrier((cross, gram))
    cross = lax.psum_scatter(cross, "z", scatter_dimension=0, tiled=True)
    gram = gram[:, : STRIP * LANE]
    inverse = swept(place, gram, swap(gram, "core"))
    cross, inverse = lax.optimization_barrier((cross, inverse))
    half = cross.shape[0] // 2
    return solve(cross[:half], swap(cross[half:], "y_hi"), split_rows(inverse))


def solution(mesh):
    names = tuple(name for name, _ in AXES)
    fine = Mesh(mesh.devices.reshape([size for _, size in AXES]), names)
    in_specs = (P(TOK, CH), P(TOK, CH), P(None, CH))
    out_specs = P(TOK + CH, None)
    return jax.shard_map(shards, mesh=fine, in_specs=in_specs, out_specs=out_specs, check_vma=False)
```
